32 devices in a mesh: dp: 16 (over z, y, x), rollout: 2 (over core).
Axes of the slice: x: 2, y: 2, z: 4, core: 2. Of those that a mesh axis runs over, the one named last changes fastest.
Arguments:
- layer_inputs: bfloat16 [2, 12288, 128], P('rollout', 'dp'), may hold values from -6 to 6
- cotangent: bfloat16 [2, 12288, 2048], P('rollout', 'dp'), may hold values from -0.0546875 to 0.0546875
- master: float32 [2, 128, 2048], P('rollout', 'dp'), may hold values from -6 to 6
- first_moment: float32 [2, 128, 2048], P('rollout', 'dp'), may hold values from -6 to 6
- second_moment: float32 [2, 128, 2048], P('rollout', 'dp'), may hold values from 0.01 to 4
- step_count: int32 [2], P('rollout'), may hold values from 1 to 1999
- bucket_owner: int32 [2], replicated, may hold values from 0 to 1, each once
Outputs:
- new_master: float32 [2, 128, 2048], P('rollout', 'dp')
- new_first: float32 [2, 128, 2048], P('rollout', 'dp')
- new_second: float32 [2, 128, 2048], P('rollout', 'dp')
- published: bfloat16 [2, 128, 2048], P(None, 'dp')
The draws below stay inside these ranges and needn't reach their ends.
Inputs may be any that keep to these rules, and one draw needn't show every extreme that they name: `bucket_owner`: each group is named once.
All inputs are finite; a program needn't handle non-finite values.
Results may differ from the reference program's by a relative error of at most 0.001.
Values may be sent and summed in bfloat16 or wider, within the bound.
No kernel may reach another device: no remote copies, remote signals or barrier semaphores. Data moves between devices by JAX's collectives and lax.ppermute only.
A program may use at most 64 MiB of HBM per device.

```python
import math
import jax
import jax.numpy as jnp
from jax import lax

FF = 2048
TOK_DEV = 768
ROWS = 128
TOKENS = 12288
N_DP = 16
N_ROLLOUT = 2


def steps_of(rng, shape, pieces, low, high):
    def one(dim, blocks):
        draws = jax.random.uniform(jax.random.fold_in(jax.random.fold_in(rng, 6), dim), (blocks,), jnp.float32, low / len(pieces), high / len(pieces))
        return jnp.repeat(jnp.exp(draws), shape[dim] // blocks).reshape((-1,) + (1,) * (len(shape) - dim - 1))

    gain = one(*pieces[0])
    for cut in pieces[1:]:
        gain = gain * one(*cut)
    return gain


def noise(rng, extent, spread, bound, split=(), kind=jnp.bfloat16):
    gain = steps_of(rng, extent, split, -0.22, 0.18) if split else 1.0
    array = jax.random.normal(rng, extent, jnp.float32) * spread * gain
    return jnp.minimum(jnp.maximum(array, -bound), bound).astype(kind)


def setup_inputs(seed: int = 0) -> dict:
    keys = jax.random.split(jax.random.key(seed), 8)
    return {
        "layer_inputs": noise(keys[0], (N_ROLLOUT, TOKENS, ROWS), 1.0, 6.0, ((0, 2), (1, 16))),
        "cotangent": noise(keys[1], (N_ROLLOUT, TOKENS, FF), TOKENS ** -0.5, 0.0546875, ((0, 2), (1, 16))),
        "master": noise(keys[2], (N_ROLLOUT, ROWS, FF), 1.0, 6.0, ((0, 2), (1, 16)), jnp.float32),
        "first_moment": noise(keys[3], (N_ROLLOUT, ROWS, FF), 1.0, 6.0, ((0, 2), (1, 16)), jnp.float32),
        "second_moment": jnp.clip(jnp.exp(math.log(4.0) - 5.9914646 * jax.random.uniform(keys[4], (N_ROLLOUT, ROWS, FF), jnp.float32) ** steps_of(keys[4], (N_ROLLOUT, ROWS, FF), ((0, 2), (1, 16)), -0.2, 0.2)), 0.01, 4.0),
        "step_count": jax.random.randint(keys[5], (N_ROLLOUT,), 1, 2000).astype(jnp.int32),
        "bucket_owner": jax.random.permutation(keys[6], N_ROLLOUT).astype(jnp.int32),
    }


def group_grad(pair):
    left, right = pair
    left = left.reshape(N_DP, TOK_DEV, ROWS)
    right = right.reshape(N_DP, TOK_DEV, FF)

    def add_shard(total, piece):
        first, second = piece
        term = lax.dot_general(first.astype(jnp.float32), second.astype(jnp.float32), (((0,), (0,)), ((), ())), precision=lax.Precision.HIGHEST)
        rounded = lax.optimization_barrier(term.astype(jnp.bfloat16)).astype(jnp.float32)
        return (total + rounded, None)
    total, unused = lax.scan(add_shard, jnp.zeros((ROWS, FF), jnp.float32), (left, right))
    return total

def reference(layer_inputs, cotangent, master, first_moment, second_moment, step_count, bucket_owner):
    grad = lax.map(group_grad, (layer_inputs, cotangent))
    new_first = 0.9 * first_moment + 0.1 * grad
    new_second = 0.999 * second_moment + 0.001 * grad * grad
    counts = (step_count + 1).astype(jnp.float32)[:, None, None]
    corr_one = 1.0 - jnp.power(jnp.float32(0.9), counts)
    corr_two = 1.0 - jnp.power(jnp.float32(0.999), counts)
    update = new_first / corr_one / (jnp.sqrt(new_second / corr_two) + 1e-08) + 0.1 * master
    new_master = master - 0.02 * update
    published = jnp.take(new_master.astype(jnp.bfloat16), bucket_owner.astype(jnp.int32), axis=0)
    return (new_master, new_first, new_second, published)
```

```python
import functools
import jax
import jax.numpy as jnp
from jax import lax
from jax.sharding import PartitionSpec as P


def rounded_term(features, upstream):
    term = lax.dot_general(
        features, upstream, (((0,), (0,)), ((), ())), preferred_element_type=jnp.float32
    )
    return lax.optimization_barrier(term.astype(jnp.bfloat16))


def tail(grad, master, first_moment, second_moment, step_count, bucket_owner, n_ro):
    grad = grad[None]
    new_first = 0.9 * first_moment + 0.1 * grad
    new_second = 0.999 * second_moment + 0.001 * grad * grad
    counts = (step_count + 1).astype(jnp.float32)[:, None, None]
    corr_one = 1.0 - jnp.power(jnp.float32(0.9), counts)
    corr_two = 1.0 - jnp.power(jnp.float32(0.999), counts)
    update = new_first / corr_one / (jnp.sqrt(new_second / corr_two) + 1e-08) + 0.1 * master
    new_master = master - 0.02 * update
    rounded = new_master.astype(jnp.bfloat16)
    if n_ro == 2:
        other = lax.ppermute(rounded, "rollout", [(0, 1), (1, 0)])
        mine = (bucket_owner == lax.axis_index("rollout"))[:, None, None]
        published = jnp.where(mine, rounded, other)
    else:
        every_group = lax.all_gather(rounded, "rollout", axis=0, tiled=True)
        published = jnp.take(every_group, bucket_owner, axis=0)
    return (new_master, new_first, new_second, published)

def total(blocks):
    acc = None
    for b in blocks:
        b = b.astype(jnp.float32)
        acc = b if acc is None else acc + b
    return acc

def solution(mesh):
    n_dp = mesh.shape["dp"]
    n_ro = mesh.shape["rollout"]
    def per_device(layer_inputs, cotangent, master, first_moment, second_moment, step_count, bucket_owner):
        partial = rounded_term(layer_inputs[0], cotangent[0])
        grad = reduce(partial, n_dp)
        return tail(grad, master, first_moment, second_moment, step_count, bucket_owner, n_ro)
    s = P("rollout", "dp", None)
    return jax.shard_map(
        per_device, mesh=mesh, in_specs=(s, s, s, s, s, P("rollout"), P()), out_specs=(s, s, s, P(None, "dp", None)), check_vma=False
    )
def reduce(partial, n):
    rows = partial.shape[0] // n
    r = lax.all_to_all(partial.reshape(n, rows, -1), "dp", 0, 0, tiled=True)
    return total([r[i] for i in range(n)])
```

```python
import functools
import jax
import jax.numpy as jnp
from jax import lax
from jax.experimental import pallas as pl
from jax.experimental.pallas import tpu as pltpu
from jax.sharding import PartitionSpec as P

VMEM_SPEC = pl.BlockSpec(memory_space=pltpu.VMEM)


def product_kernel(inner, outer, chunks, features_hbm, upstream_hbm, *refs):
    blocks, (features_ref, upstream, product, sems) = refs[:inner], refs[inner:]
    ff = upstream.shape[1]
    width = ff // chunks
    rows = product.shape[0] // (inner * outer)
    first = pltpu.make_async_copy(features_hbm, features_ref, sems.at[chunks])
    first.start()
    copies = []
    for c in range(chunks):
        cols = pl.ds(c * width, width)
        copy = pltpu.make_async_copy(upstream_hbm.at[:, cols], upstream.at[:, cols], sems.at[c])
        copy.start()
        copies.append(copy)
    mine = lax.rem(lax.axis_index("dp"), inner)
    first.wait()
    for c in range(chunks):
        cols = slice(c * width, (c + 1) * width)
        copies[c].wait()
        product[:, cols] = lax.dot_general(
            features_ref[...], upstream[:, cols], (((0,), (0,)), ((), ())), preferred_element_type=jnp.float32
        )
        for d in range(inner):
            peer = jnp.bitwise_xor(mine, d)
            parts = [
                product[pl.ds(pl.multiple_of((o * inner + peer) * rows, rows), rows), cols] for o in range(outer)
            ]
            blocks[d][:, cols] = jnp.concatenate(parts, axis=0).astype(jnp.bfloat16)


def product_blocks(features, upstream, inner, outer):
    tokens, rows = features.shape
    ff = upstream.shape[1]
    chunks = 2 if ff % 256 == 0 else 1
    block = pltpu.VMEM((rows // inner, ff), jnp.bfloat16)
    return pl.pallas_call(
        functools.partial(product_kernel, inner, outer, chunks),
        out_shape=[block] * inner,
        in_specs=[pl.BlockSpec(memory_space=pltpu.HBM)] * 2,
        out_specs=[VMEM_SPEC] * inner,
        scratch_shapes=[
            pltpu.VMEM((tokens, rows), jnp.bfloat16),
            pltpu.VMEM((tokens, ff), jnp.bfloat16),
            pltpu.VMEM((rows, ff), jnp.float32),
            pltpu.SemaphoreType.DMA((chunks + 1,)),
        ],
        compiler_params=pltpu.CompilerParams(vmem_limit_bytes=24 * 2**20),
        name="product",
    )(*(pltpu.with_memory_space_constraint(x, pltpu.HBM) for x in (features, upstream)))


def middle_kernel(inner, outer, *refs):
    got, sent, total = refs[:inner], refs[inner : inner + outer], refs[-1]
    acc = got[0][...].astype(jnp.float32)
    for g in got[1:]:
        acc = acc + g[...].astype(jnp.float32)
    total[...] = acc
    rows = total.shape[0] // outer
    mine = lax.axis_index("dp") // inner
    for d in range(outer):
        peer = jnp.bitwise_xor(mine, d)
        sent[d][...] = total[pl.ds(pl.multiple_of(peer * rows, rows), rows), :].astype(sent[d].dtype)


def middle_sums(got, inner, outer):
    rows, ff = got[0].shape
    part = pltpu.VMEM((rows // outer, ff), jnp.float32)
    got = [pltpu.with_memory_space_constraint(g, pltpu.VMEM) for g in got]
    return pl.pallas_call(
        functools.partial(middle_kernel, inner, outer),
        out_shape=[part] * outer,
        in_specs=[VMEM_SPEC] * inner,
        out_specs=[VMEM_SPEC] * outer,
        scratch_shapes=[pltpu.VMEM((rows, ff), jnp.float32)],
        compiler_params=pltpu.CompilerParams(vmem_limit_bytes=8 * 2**20),
        name="middle",
    )(*got)


def total(blocks):
    acc = None
    for b in blocks:
        b = b.astype(jnp.float32)
        acc = b if acc is None else acc + b
    return acc


def split_of(n):
    inner = 1
    while inner * inner < n:
        inner *= 2
    return inner, n // inner


def swap(blocks, stride, n):
    far = len(blocks) - 1
    got = {0: blocks[0]}
    for d in [far, *range(1, far)]:
        got[d] = lax.ppermute(blocks[d], "dp", [(i, i ^ (d * stride)) for i in range(n)])
    return list(got.values())


def solution(mesh):
    n_dp = mesh.shape["dp"]
    n_ro = mesh.shape["rollout"]

    def per_device(layer_inputs, cotangent, master, first_moment, second_moment, step_count, bucket_owner):
        inner, outer = split_of(n_dp)
        blocks = product_blocks(layer_inputs[0], cotangent[0], inner, outer)
        parts = middle_sums(swap(blocks, 1, n_dp), inner, outer)
        grad = total(swap(parts, inner, n_dp))
        return tail(grad, master, first_moment, second_moment, step_count, bucket_owner, n_ro)

    s = P("rollout", "dp", None)
    return jax.shard_map(
        per_device, mesh=mesh, in_specs=(s, s, s, s, s, P("rollout"), P()), out_specs=(s, s, s, P(None, "dp", None)), check_vma=False
    )


def tail(grad, master, first_moment, second_moment, step_count, bucket_owner, n_ro):
    grad = grad[None]
    new_first = 0.9 * first_moment + 0.1 * grad
    new_second = 0.999 * second_moment + 0.001 * grad * grad
    counts = (step_count + 1).astype(jnp.float32)[:, None, None]
    corr_one = 1.0 - jnp.power(jnp.float32(0.9), counts)
    corr_two = 1.0 - jnp.power(jnp.float32(0.999), counts)
    update = new_first / corr_one / (jnp.sqrt(new_second / corr_two) + 1e-08) + 0.1 * master
    new_master = master - 0.02 * update
    rounded = new_master.astype(jnp.bfloat16)
    if n_ro == 2:
        other = lax.ppermute(rounded, "rollout", [(0, 1), (1, 0)])
        mine = (bucket_owner == lax.axis_index("rollout"))[:, None, None]
        published = jnp.where(mine, rounded, other)
    else:
        every_group = lax.all_gather(rounded, "rollout", axis=0, tiled=True)
        published = jnp.take(every_group, bucket_owner, axis=0)
    return (new_master, new_first, new_second, published)
```

```python
import functools
import jax
import jax.numpy as jnp
from jax import lax
from jax.experimental import pallas as pl
from jax.experimental.pallas import tpu as pltpu
from jax.sharding import PartitionSpec as P

VMEM_SPEC = pl.BlockSpec(memory_space=pltpu.VMEM)


def turned_here(inner, outer):
    return (lax.axis_index("rollout") % 2 == 1) if inner == outer else (lax.axis_index("rollout") < 0)


def distance(step, count):
    return 0 if step == 0 else (step + count - 3) % (count - 1) + 1


def product_kernel(inner, outer, chunks, features_hbm, upstream_hbm, *refs):
    blocks, (features, upstream, product, sems) = refs[:inner], refs[inner:]
    depth = upstream.shape[0] // chunks
    rows = product.shape[0] // (inner * outer)
    copies = []
    for c in range(chunks):
        part = pl.ds(c * depth, depth)
        pair = (
            pltpu.make_async_copy(features_hbm.at[part], features.at[part], sems.at[c, 0]),
            pltpu.make_async_copy(upstream_hbm.at[part], upstream.at[part], sems.at[c, 1]),
        )
        for copy in pair:
            copy.start()
        copies.append(pair)
    turned = turned_here(inner, outer)
    mine = jnp.where(turned, lax.axis_index("dp") // inner, lax.rem(lax.axis_index("dp"), inner))
    peer_step = jnp.where(turned, inner, 1)
    other_step = jnp.where(turned, 1, inner)
    for c in range(chunks):
        part = slice(c * depth, (c + 1) * depth)
        for copy in copies[c]:
            copy.wait()
        term = lax.dot_general(
            features[part], upstream[part], (((0,), (0,)), ((), ())), preferred_element_type=jnp.float32
        )
        product[...] = term if c == 0 else product[...] + term
    for d in range(inner):
        peer = jnp.bitwise_xor(mine, distance(d, inner))
        for o in range(0, outer, 2):
            places = [((o + i) * other_step + peer * peer_step) * rows for i in range(2)]
            parts = [product[pl.ds(pl.multiple_of(at, rows), rows), :] for at in places]
            blocks[d][o * rows : (o + 2) * rows] = jnp.concatenate(parts, axis=0).astype(jnp.bfloat16)


def product_blocks(features, upstream, inner, outer):
    tokens, rows = features.shape
    ff = upstream.shape[1]
    chunks = 3 if tokens % 384 == 0 else 1
    block = pltpu.VMEM((rows // inner, ff), jnp.bfloat16)
    return pl.pallas_call(
        functools.partial(product_kernel, inner, outer, chunks),
        out_shape=[block] * inner,
        in_specs=[pl.BlockSpec(memory_space=pltpu.HBM)] * 2,
        out_specs=[VMEM_SPEC] * inner,
        scratch_shapes=[
            pltpu.VMEM((tokens, rows), jnp.bfloat16),
            pltpu.VMEM((tokens, ff), jnp.bfloat16),
            pltpu.VMEM((rows, ff), jnp.float32),
            pltpu.SemaphoreType.DMA((chunks, 2)),
        ],
        compiler_params=pltpu.CompilerParams(vmem_limit_bytes=24 * 2**20),
        name="product",
    )(*(pltpu.with_memory_space_constraint(x, pltpu.HBM) for x in (features, upstream)))


def middle_kernel(inner, outer, *refs):
    got, sent, total = refs[:inner], refs[inner : inner + outer], refs[-1]
    acc = got[0][...].astype(jnp.float32)
    for g in got[1:]:
        acc = acc + g[...].astype(jnp.float32)
    total[...] = acc
    rows = total.shape[0] // outer
    turned = turned_here(inner, outer)
    mine = jnp.where(turned, lax.rem(lax.axis_index("dp"), inner), lax.axis_index("dp") // inner)
    for d in range(outer):
        peer = jnp.bitwise_xor(mine, distance(d, outer))
        sent[d][...] = total[pl.ds(pl.multiple_of(peer * rows, rows), rows), :].astype(sent[d].dtype)


def middle_sums(got, inner, outer):
    rows, ff = got[0].shape
    part = pltpu.VMEM((rows // outer, ff), jnp.float32)
    got = [pltpu.with_memory_space_constraint(g, pltpu.VMEM) for g in got]
    return pl.pallas_call(
        functools.partial(middle_kernel, inner, outer),
        out_shape=[part] * outer,
        in_specs=[VMEM_SPEC] * inner,
        out_specs=[VMEM_SPEC] * outer,
        scratch_shapes=[pltpu.VMEM((rows, ff), jnp.float32)],
        compiler_params=pltpu.CompilerParams(vmem_limit_bytes=8 * 2**20),
        name="middle",
    )(*got)


def stepped(grad, first, second, master, step):
    new_first = 0.9 * first[0] + 0.1 * grad
    new_second = 0.999 * second[0] + 0.001 * grad * grad
    update = new_first / step[0] / (jnp.sqrt(new_second / step[1]) + 1e-08) + 0.1 * master[0]
    return master[0] - 0.02 * update, new_first, new_second


def publish_kernel(n_parts, *refs):
    parts, state, (grad, rounded) = refs[:n_parts], refs[n_parts:-2], refs[-2:]
    acc = parts[0][...].astype(jnp.float32)
    for p in parts[1:]:
        acc = acc + p[...].astype(jnp.float32)
    grad[...] = acc
    rounded[0] = stepped(acc, *state)[0].astype(jnp.bfloat16)


def store_kernel(grad, first, second, master, step, *refs):
    outs, (held, sems) = refs[:3], refs[3:]
    copies = []
    for k, value in enumerate(stepped(grad[...], first, second, master, step)):
        held[k] = value
        copy = pltpu.make_async_copy(held.at[k], outs[k].at[0], sems.at[k])
        copy.start()
        copies.append(copy)
    for copy in copies:
        copy.wait()


def held_in_vmem(arrays):
    return [pltpu.with_memory_space_constraint(x, pltpu.VMEM) for x in arrays]


def to_publish(parts, state):
    shape = state[0].shape
    args = held_in_vmem((*parts, *state))
    return pl.pallas_call(
        functools.partial(publish_kernel, len(parts)),
        out_shape=[pltpu.VMEM(shape[1:], jnp.float32), pltpu.VMEM(shape, jnp.bfloat16)],
        in_specs=[VMEM_SPEC] * len(args),
        out_specs=[VMEM_SPEC] * 2,
        compiler_params=pltpu.CompilerParams(vmem_limit_bytes=8 * 2**20),
        name="publish",
    )(*args)


def stored(grad, state):
    shape = state[0].shape
    args = held_in_vmem((grad, *state))
    return pl.pallas_call(
        store_kernel,
        out_shape=[jax.ShapeDtypeStruct(shape, jnp.float32)] * 3,
        in_specs=[VMEM_SPEC] * len(args),
        out_specs=[pl.BlockSpec(memory_space=pltpu.HBM)] * 3,
        scratch_shapes=[pltpu.VMEM((3, *shape[1:]), jnp.float32), pltpu.SemaphoreType.DMA((3,))],
        compiler_params=pltpu.CompilerParams(vmem_limit_bytes=8 * 2**20),
        cost_estimate=pl.CostEstimate(flops=2**20, bytes_accessed=2**20, transcendentals=0),
        name="store",
    )(*args)


def split_of(n):
    inner = 1
    while inner * inner < n:
        inner *= 2
    return inner, n // inner


def swap(blocks, strides, n, n_ro):
    count = len(blocks)
    got = [blocks[0]]
    for step in range(1, count):
        pairs = []
        for i in range(n):
            for r in range(n_ro):
                turned = r % 2 if strides[0] != strides[1] else 0
                pairs.append((i * n_ro + r, (i ^ (distance(step, count) * strides[turned])) * n_ro + r))
        got.append(lax.ppermute(blocks[step], ("dp", "rollout"), pairs))
    return got


def solution(mesh):
    n_dp = mesh.shape["dp"]
    n_ro = mesh.shape["rollout"]

    def per_device(layer_inputs, cotangent, master, first_moment, second_moment, step_count, bucket_owner):
        inner, outer = split_of(n_dp)
        strides = (1, inner) if inner == outer else (1, 1)
        blocks = product_blocks(layer_inputs[0], cotangent[0], inner, outer)
        parts = middle_sums(swap(blocks, strides, n_dp, n_ro), inner, outer)
        counts = (step_count + 1).astype(jnp.float32)
        corrections = 1.0 - jnp.power(jnp.array([0.9, 0.999], jnp.float32), counts)
        state = (first_moment, second_moment, master, corrections[:, None, None])
        grad, rounded = to_publish(swap(parts, strides[::-1], n_dp, n_ro), state)
        new_master, new_first, new_second = stored(grad, state)
        if n_ro == 2:
            other = lax.ppermute(rounded, "rollout", [(0, 1), (1, 0)])
            published = jnp.where((bucket_owner == lax.axis_index("rollout"))[:, None, None], rounded, other)
        else:
            every_group = lax.all_gather(rounded, "rollout", axis=0, tiled=True)
            published = jnp.take(every_group, bucket_owner, axis=0)
        return new_master, new_first, new_second, published

    s = P("rollout", "dp", None)
    return jax.shard_map(
        per_device, mesh=mesh, in_specs=(s, s, s, s, s, P("rollout"), P()), out_specs=(s, s, s, P(None, "dp", None)), check_vma=False
    )
```

```python
import functools
import jax
import jax.numpy as jnp
from jax import lax
from jax.experimental import pallas as pl
from jax.experimental.pallas import tpu as pltpu
from jax.sharding import PartitionSpec as P

VMEM_SPEC = pl.BlockSpec(memory_space=pltpu.VMEM)


def turned_here(inner, outer):
    return (lax.axis_index("rollout") % 2 == 1) if inner == outer else (lax.axis_index("rollout") < 0)


def plane_peer(mine, step, count):
    return mine ^ (0 if step == 0 else (step + count - 3) % (count - 1) + 1)


def line_peer(mine, step, count):
    return (mine + step) & (count - 1)


def product_kernel(inner, outer, cuts, features_hbm, upstream_hbm, *refs):
    blocks, (features, upstream, product, sems) = refs[:inner], refs[inner:]
    chunks = len(cuts) - 1
    rows = product.shape[0] // (inner * outer)
    copies = []
    for c in range(chunks):
        part = pl.ds(cuts[c], cuts[c + 1] - cuts[c])
        pair = (
            pltpu.make_async_copy(features_hbm.at[part], features.at[part], sems.at[c, 0]),
            pltpu.make_async_copy(upstream_hbm.at[part], upstream.at[part], sems.at[c, 1]),
        )
        for copy in pair:
            copy.start()
        copies.append(pair)
    turned = turned_here(inner, outer)
    mine = jnp.where(turned, lax.axis_index("dp") // inner, lax.rem(lax.axis_index("dp"), inner))
    peer_step = jnp.where(turned, inner, 1)
    other_step = jnp.where(turned, 1, inner)
    for c in range(chunks):
        part = slice(cuts[c], cuts[c + 1])
        for copy in copies[c]:
            copy.wait()
        term = lax.dot_general(
            features[part], upstream[part], (((0,), (0,)), ((), ())), preferred_element_type=jnp.float32
        )
        product[...] = term if c == 0 else product[...] + term
    for d in range(inner):
        peer = jnp.where(turned, line_peer(mine, d, inner), plane_peer(mine, d, inner))
        for o in range(0, outer, 2):
            places = [((o + i) * other_step + peer * peer_step) * rows for i in range(2)]
            parts = [product[pl.ds(pl.multiple_of(at, rows), rows), :] for at in places]
            blocks[d][o * rows : (o + 2) * rows] = jnp.concatenate(parts, axis=0).astype(jnp.bfloat16)


def product_blocks(features, upstream, inner, outer):
    tokens, rows = features.shape
    ff = upstream.shape[1]
    shares = [0, 1, 2, 3]
    unit = tokens // shares[-1]
    cuts = [share * unit for share in shares] if tokens % (16 * shares[-1]) == 0 else [0, tokens]
    block = pltpu.VMEM((rows // inner, ff), jnp.bfloat16)
    return pl.pallas_call(
        functools.partial(product_kernel, inner, outer, cuts),
        out_shape=[block] * inner,
        in_specs=[pl.BlockSpec(memory_space=pltpu.HBM)] * 2,
        out_specs=[VMEM_SPEC] * inner,
        scratch_shapes=[
            pltpu.VMEM((tokens, rows), jnp.bfloat16),
            pltpu.VMEM((tokens, ff), jnp.bfloat16),
            pltpu.VMEM((rows, ff), jnp.float32),
            pltpu.SemaphoreType.DMA((len(cuts) - 1, 2)),
        ],
        compiler_params=pltpu.CompilerParams(vmem_limit_bytes=24 * 2**20),
        name="product",
    )(*(pltpu.with_memory_space_constraint(x, pltpu.HBM) for x in (features, upstream)))


def middle_kernel(inner, outer, *refs):
    got, sent, total = refs[:inner], refs[inner : inner + outer], refs[-1]
    acc = got[0][...].astype(jnp.float32)
    for g in got[1:]:
        acc = acc + g[...].astype(jnp.float32)
    total[...] = acc
    rows = total.shape[0] // outer
    turned = turned_here(inner, outer)
    mine = jnp.where(turned, lax.rem(lax.axis_index("dp"), inner), lax.axis_index("dp") // inner)
    for d in range(outer):
        peer = jnp.where(turned, plane_peer(mine, d, outer), line_peer(mine, d, outer))
        sent[d][...] = total[pl.ds(pl.multiple_of(peer * rows, rows), rows), :].astype(sent[d].dtype)


def middle_sums(got, inner, outer):
    rows, ff = got[0].shape
    part = pltpu.VMEM((rows // outer, ff), jnp.float32)
    got = [pltpu.with_memory_space_constraint(g, pltpu.VMEM) for g in got]
    return pl.pallas_call(
        functools.partial(middle_kernel, inner, outer),
        out_shape=[part] * outer,
        in_specs=[VMEM_SPEC] * inner,
        out_specs=[VMEM_SPEC] * outer,
        scratch_shapes=[pltpu.VMEM((rows, ff), jnp.float32)],
        compiler_params=pltpu.CompilerParams(vmem_limit_bytes=8 * 2**20),
        name="middle",
    )(*got)


def stepped(grad, first, second, master, step):
    new_first = 0.9 * first[0] + 0.1 * grad
    new_second = 0.999 * second[0] + 0.001 * grad * grad
    update = new_first / step[0] / (jnp.sqrt(new_second / step[1]) + 1e-08) + 0.1 * master[0]
    return master[0] - 0.02 * update, new_first, new_second


def publish_kernel(n_parts, *refs):
    parts, state, (grad, rounded) = refs[:n_parts], refs[n_parts:-2], refs[-2:]
    acc = parts[0][...].astype(jnp.float32)
    for p in parts[1:]:
        acc = acc + p[...].astype(jnp.float32)
    grad[...] = acc
    rounded[0] = stepped(acc, *state)[0].astype(jnp.bfloat16)


def store_kernel(grad, first, second, master, step, *refs):
    outs, (held, sems) = refs[:3], refs[3:]
    copies = []
    for k, value in enumerate(stepped(grad[...], first, second, master, step)):
        held[k] = value
        copy = pltpu.make_async_copy(held.at[k], outs[k].at[0], sems.at[k])
        copy.start()
        copies.append(copy)
    for copy in copies:
        copy.wait()


def held_in_vmem(arrays):
    return [pltpu.with_memory_space_constraint(x, pltpu.VMEM) for x in arrays]


def to_publish(parts, state):
    shape = state[0].shape
    args = held_in_vmem((*parts, *state))
    return pl.pallas_call(
        functools.partial(publish_kernel, len(parts)),
        out_shape=[pltpu.VMEM(shape[1:], jnp.float32), pltpu.VMEM(shape, jnp.bfloat16)],
        in_specs=[VMEM_SPEC] * len(args),
        out_specs=[VMEM_SPEC] * 2,
        compiler_params=pltpu.CompilerParams(vmem_limit_bytes=8 * 2**20),
        name="publish",
    )(*args)


def stored(grad, state):
    shape = state[0].shape
    args = held_in_vmem((grad, *state))
    return pl.pallas_call(
        store_kernel,
        out_shape=[jax.ShapeDtypeStruct(shape, jnp.float32)] * 3,
        in_specs=[VMEM_SPEC] * len(args),
        out_specs=[pl.BlockSpec(memory_space=pltpu.HBM)] * 3,
        scratch_shapes=[pltpu.VMEM((3, *shape[1:]), jnp.float32), pltpu.SemaphoreType.DMA((3,))],
        compiler_params=pltpu.CompilerParams(vmem_limit_bytes=8 * 2**20),
        cost_estimate=pl.CostEstimate(flops=2**20, bytes_accessed=2**20, transcendentals=0),
        name="store",
    )(*args)


def split_of(n):
    inner = 1
    while inner * inner < n:
        inner *= 2
    return inner, n // inner


def swap(blocks, level, inner, n, n_ro):
    count = len(blocks)
    got = [blocks[0]]
    for step in range(1, count):
        pairs = []
        for i in range(n):
            for r in range(n_ro):
                turned = r % 2 == 1 and inner * inner == n
                line = turned if level == 1 else not turned
                stride, rule = (inner, line_peer if level == 1 else line_peer) if line else (1, plane_peer)
                mine = i // stride % count
                to = i + (rule(mine, step, count) - mine) * stride
                pairs.append((i * n_ro + r, to * n_ro + r))
        got.append(lax.ppermute(blocks[step], ("dp", "rollout"), pairs))
    return got


def solution(mesh):
    n_dp = mesh.shape["dp"]
    n_ro = mesh.shape["rollout"]

    def per_device(layer_inputs, cotangent, master, first_moment, second_moment, step_count, bucket_owner):
        inner, outer = split_of(n_dp)
        blocks = product_blocks(layer_inputs[0], cotangent[0], inner, outer)
        parts = middle_sums(swap(blocks, 1, inner, n_dp, n_ro), inner, outer)
        counts = (step_count + 1).astype(jnp.float32)
        corrections = 1.0 - jnp.power(jnp.array([0.9, 0.999], jnp.float32), counts)
        state = (first_moment, second_moment, master, corrections[:, None, None])
        grad, rounded = to_publish(swap(parts, 2, inner, n_dp, n_ro), state)
        new_master, new_first, new_second = stored(grad, state)
        if n_ro == 2:
            other = lax.ppermute(rounded, "rollout", [(0, 1), (1, 0)])
            published = jnp.where((bucket_owner == lax.axis_index("rollout"))[:, None, None], rounded, other)
        else:
            every_group = lax.all_gather(rounded, "rollout", axis=0, tiled=True)
            published = jnp.take(every_group, bucket_owner, axis=0)
        return new_master, new_first, new_second, published

    s = P("rollout", "dp", None)
    return jax.shard_map(
        per_device, mesh=mesh, in_specs=(s, s, s, s, s, P("rollout"), P()), out_specs=(s, s, s, P(None, "dp", None)), check_vma=False
    )
```

```python
import functools
import jax
import jax.numpy as jnp
from jax import lax
from jax.experimental import pallas as pl
from jax.experimental.pallas import tpu as pltpu
from jax.sharding import PartitionSpec as P

VMEM_SPEC = pl.BlockSpec(memory_space=pltpu.VMEM)


def turned_here(inner, outer):
    return (lax.axis_index("rollout") % 2 == 1) if inner == outer else (lax.axis_index("rollout") < 0)


def plane_peer(mine, step, count):
    return mine ^ (0 if step == 0 else (step + count - 3) % (count - 1) + 1)


def line_peer(mine, step, count):
    if count != 4:
        return (mine + step) & (count - 1)
    place = (mine & 1) * 2 + (mine >> 1)
    to = (place + (0, 1, 3, 2)[step]) & 3
    return (to & 1) * 2 + (to >> 1)


def product_kernel(inner, outer, cuts, features_hbm, upstream_hbm, *refs):
    blocks, (features, upstream, product, sems) = refs[:inner], refs[inner:]
    chunks = len(cuts) - 1
    rows = product.shape[0] // (inner * outer)
    copies = []
    for c in range(chunks):
        part = pl.ds(cuts[c], cuts[c + 1] - cuts[c])
        pair = (
            pltpu.make_async_copy(features_hbm.at[part], features.at[part], sems.at[c, 0]),
            pltpu.make_async_copy(upstream_hbm.at[part], upstream.at[part], sems.at[c, 1]),
        )
        for copy in pair:
            copy.start()
        copies.append(pair)
    turned = turned_here(inner, outer)
    mine = jnp.where(turned, lax.axis_index("dp") // inner, lax.rem(lax.axis_index("dp"), inner))
    peer_step = jnp.where(turned, inner, 1)
    other_step = jnp.where(turned, 1, inner)
    for c in range(chunks):
        part = slice(cuts[c], cuts[c + 1])
        for copy in copies[c]:
            copy.wait()
        term = lax.dot_general(
            features[part], upstream[part], (((0,), (0,)), ((), ())), preferred_element_type=jnp.float32
        )
        product[...] = term if c == 0 else product[...] + term
    for d in range(inner):
        peer = jnp.where(turned, line_peer(mine, d, inner), plane_peer(mine, d, inner))
        for o in range(0, outer, 2):
            places = [((o + i) * other_step + peer * peer_step) * rows for i in range(2)]
            parts = [product[pl.ds(pl.multiple_of(at, rows), rows), :] for at in places]
            blocks[d][o * rows : (o + 2) * rows] = jnp.concatenate(parts, axis=0).astype(jnp.bfloat16)


def product_blocks(features, upstream, inner, outer):
    tokens, rows = features.shape
    ff = upstream.shape[1]
    shares = [0, 1, 2, 3]
    unit = tokens // shares[-1]
    cuts = [share * unit for share in shares] if tokens % (16 * shares[-1]) == 0 else [0, tokens]
    block = pltpu.VMEM((rows // inner, ff), jnp.bfloat16)
    return pl.pallas_call(
        functools.partial(product_kernel, inner, outer, cuts),
        out_shape=[block] * inner,
        in_specs=[pl.BlockSpec(memory_space=pltpu.HBM)] * 2,
        out_specs=[VMEM_SPEC] * inner,
        scratch_shapes=[
            pltpu.VMEM((tokens, rows), jnp.bfloat16),
            pltpu.VMEM((tokens, ff), jnp.bfloat16),
            pltpu.VMEM((rows, ff), jnp.float32),
            pltpu.SemaphoreType.DMA((len(cuts) - 1, 2)),
        ],
        compiler_params=pltpu.CompilerParams(vmem_limit_bytes=24 * 2**20),
        name="product",
    )(*(pltpu.with_memory_space_constraint(x, pltpu.HBM) for x in (features, upstream)))


def middle_kernel(inner, outer, packs, *refs):
    got, state, sent, total = refs[:inner], refs[inner : inner + packs], refs[inner + packs : -1], refs[-1]
    acc = got[0][...].astype(jnp.float32)
    for g in got[1:]:
        acc = acc + g[...].astype(jnp.float32)
    total[...] = acc
    rows = total.shape[0] // outer
    turned = turned_here(inner, outer)
    mine = jnp.where(turned, lax.rem(lax.axis_index("dp"), inner), lax.axis_index("dp") // inner)
    for d in range(outer):
        peer = jnp.where(turned, plane_peer(mine, d, outer), line_peer(mine, d, outer))
        sent[d][:, : total.shape[1]] = total[pl.ds(pl.multiple_of(peer * rows, rows), rows), :].astype(sent[d].dtype)
    if packs:
        cross, ff = sent[outer - 1], total.shape[1]
        for k in range(2):
            cross[:, ff + k * 128 : ff + (k + 1) * 128] = jnp.broadcast_to(state[0][k], (rows, 128))


def middle_sums(got, inner, outer, state=()):
    rows, ff = got[0].shape
    part = pltpu.VMEM((rows // outer, ff), jnp.float32)
    packed = [pltpu.VMEM((rows // outer, ff + 256), jnp.float32)] if state else []
    args = held_in_vmem((*got, *state))
    return pl.pallas_call(
        functools.partial(middle_kernel, inner, outer, len(state)),
        out_shape=[part] * (outer - len(packed)) + packed,
        in_specs=[VMEM_SPEC] * len(args),
        out_specs=[VMEM_SPEC] * outer,
        scratch_shapes=[pltpu.VMEM((rows, ff), jnp.float32)],
        compiler_params=pltpu.CompilerParams(vmem_limit_bytes=8 * 2**20),
        name="middle",
    )(*args)


def stepped(grad, first, second, master, step):
    new_first = 0.9 * first[0] + 0.1 * grad
    new_second = 0.999 * second[0] + 0.001 * grad * grad
    update = new_first / step[0] / (jnp.sqrt(new_second / step[1]) + 1e-08) + 0.1 * master[0]
    return master[0] - 0.02 * update, new_first, new_second


def publish_kernel(n_parts, *refs):
    parts, state, (grad, rounded) = refs[:n_parts], refs[n_parts:-2], refs[-2:]
    acc = parts[0][...].astype(jnp.float32)
    for p in parts[1:]:
        acc = acc + p[...].astype(jnp.float32)
    grad[...] = acc
    rounded[0] = stepped(acc, *state)[0].astype(jnp.bfloat16)


def store_kernel(grad, first, second, master, step, *refs):
    outs, (held, sems) = refs[:3], refs[3:]
    copies = []
    for k, value in enumerate(stepped(grad[...], first, second, master, step)):
        held[k] = value
        copy = pltpu.make_async_copy(held.at[k], outs[k].at[0], sems.at[k])
        copy.start()
        copies.append(copy)
    for copy in copies:
        copy.wait()


def held_in_vmem(arrays):
    return [pltpu.with_memory_space_constraint(x, pltpu.VMEM) for x in arrays]


def to_publish(parts, state):
    shape = state[0].shape
    args = held_in_vmem((*parts, *state))
    return pl.pallas_call(
        functools.partial(publish_kernel, len(parts)),
        out_shape=[pltpu.VMEM(shape[1:], jnp.float32), pltpu.VMEM(shape, jnp.bfloat16)],
        in_specs=[VMEM_SPEC] * len(args),
        out_specs=[VMEM_SPEC] * 2,
        compiler_params=pltpu.CompilerParams(vmem_limit_bytes=8 * 2**20),
        name="publish",
    )(*args)


def stored(grad, state):
    shape = state[0].shape
    args = held_in_vmem((grad, *state))
    return pl.pallas_call(
        store_kernel,
        out_shape=[jax.ShapeDtypeStruct(shape, jnp.float32)] * 3,
        in_specs=[VMEM_SPEC] * len(args),
        out_specs=[pl.BlockSpec(memory_space=pltpu.HBM)] * 3,
        scratch_shapes=[pltpu.VMEM((3, *shape[1:]), jnp.float32), pltpu.SemaphoreType.DMA((3,))],
        compiler_params=pltpu.CompilerParams(vmem_limit_bytes=8 * 2**20),
        cost_estimate=pl.CostEstimate(flops=2**20, bytes_accessed=2**20, transcendentals=0),
        name="store",
    )(*args)


def pack_kernel(first, second, master, anchor, out):
    for k, ref in enumerate((first, second, master)):
        out[k] = ref[0]


def packed_state(state, anchor):
    return pl.pallas_call(
        pack_kernel,
        out_shape=pltpu.VMEM((3, *state[0].shape[1:]), jnp.float32),
        in_specs=[VMEM_SPEC] * 4,
        out_specs=VMEM_SPEC,
        compiler_params=pltpu.CompilerParams(vmem_limit_bytes=4 * 2**20),
        name="pack",
    )(*held_in_vmem((*state[:3], anchor)))


def partial_kernel(*refs):
    acc = refs[0][...]
    for ref in refs[1:-1]:
        acc = acc + ref[...]
    refs[-1][...] = acc


def partial_sum(parts):
    return pl.pallas_call(
        partial_kernel,
        out_shape=pltpu.VMEM(parts[0].shape, jnp.float32),
        in_specs=[VMEM_SPEC] * len(parts),
        out_specs=VMEM_SPEC,
        compiler_params=pltpu.CompilerParams(vmem_limit_bytes=4 * 2**20),
        name="partial",
    )(*held_in_vmem(parts))


def finish_kernel(
    part, last, far_part, far_last, first, second, master, step, far, mask, *refs
):
    outs, published, (held, rounded, sems) = refs[:3], refs[3], refs[4:]
    copies = []
    ours = stepped(part[...] + last[:, : part.shape[1]], first, second, master, step)
    ff = part.shape[1]
    steps = [far_last[:, ff + k * 128 : ff + k * 128 + 1] for k in range(2)]
    theirs = stepped(far_part[...] + far_last[:, :ff], far.at[0:1], far.at[1:2], far.at[2:3], steps)[0]
    here = mask[...] > 0
    rounded[0] = jnp.where(here, ours[0], theirs).astype(jnp.bfloat16)
    rounded[1] = jnp.where(here, theirs, ours[0]).astype(jnp.bfloat16)
    copies.append(pltpu.make_async_copy(rounded, published, sems.at[3]))
    copies[0].start()
    for k, value in enumerate(ours):
        held[k] = value
        copy = pltpu.make_async_copy(held.at[k], outs[k].at[0], sems.at[k])
        copy.start()
        copies.append(copy)
    for copy in copies:
        copy.wait()


def finished(part, last, far_part, far_last, state, far, mask):
    shape = state[0].shape
    args = held_in_vmem((part, last, far_part, far_last, *state, far, mask))
    return pl.pallas_call(
        finish_kernel,
        out_shape=[jax.ShapeDtypeStruct(shape, jnp.float32)] * 3
        + [jax.ShapeDtypeStruct((2, *shape[1:]), jnp.bfloat16)],
        in_specs=[VMEM_SPEC] * len(args),
        out_specs=[pl.BlockSpec(memory_space=pltpu.HBM)] * 4,
        scratch_shapes=[
            pltpu.VMEM((3, *shape[1:]), jnp.float32),
            pltpu.VMEM((2, *shape[1:]), jnp.bfloat16),
            pltpu.SemaphoreType.DMA((4,)),
        ],
        compiler_params=pltpu.CompilerParams(vmem_limit_bytes=8 * 2**20),
        name="finish",
    )(*args)


def over_cores(x):
    return lax.ppermute(x, "rollout", [(0, 1), (1, 0)])


def split_of(n):
    inner = 1
    while inner * inner < n:
        inner *= 2
    return inner, n // inner


def exchange(block, step, count, level, inner, n, n_ro, cross=0):
    pairs = []
    for i in range(n):
        for r in range(n_ro):
            turned = r % 2 == 1 and inner * inner == n
            line = turned if level == 1 else not turned
            stride, rule = (inner, line_peer) if line else (1, plane_peer)
            mine = i // stride % count
            to = i + (rule(mine, step, count) - mine) * stride
            pairs.append((i * n_ro + r, to * n_ro + (r ^ cross)))
    return lax.ppermute(block, ("dp", "rollout"), pairs)


def swap(blocks, level, inner, n, n_ro):
    count = len(blocks)
    return [blocks[0]] + [exchange(blocks[k], k, count, level, inner, n, n_ro) for k in range(1, count)]


def solution(mesh):
    n_dp = mesh.shape["dp"]
    n_ro = mesh.shape["rollout"]

    def per_device(layer_inputs, cotangent, master, first_moment, second_moment, step_count, bucket_owner):
        inner, outer = split_of(n_dp)
        blocks = product_blocks(layer_inputs[0], cotangent[0], inner, outer)
        got = swap(blocks, 1, inner, n_dp, n_ro)
        counts = (step_count + 1).astype(jnp.float32)
        corrections = 1.0 - jnp.power(jnp.array([0.9, 0.999], jnp.float32), counts)
        state = (first_moment, second_moment, master, corrections[:, None, None])
        if n_ro != 2:
            parts = middle_sums(got, inner, outer)
            grad, rounded = to_publish(swap(parts, 2, inner, n_dp, n_ro), state)
            every_group = lax.all_gather(rounded, "rollout", axis=0, tiled=True)
            return (*stored(grad, state), jnp.take(every_group, bucket_owner, axis=0))
        parts = middle_sums(got, inner, outer, state[3:])
        mine = swap(parts, 2, inner, n_dp, n_ro)
        far_last = exchange(parts[-1], outer - 1, outer, 2, inner, n_dp, n_ro, cross=1)
        far = over_cores(packed_state(state, blocks[0]))
        part = partial_sum(mine[:-1])
        mask = jnp.full((1, 1), bucket_owner[0] == lax.axis_index("rollout"), jnp.float32)
        return tuple(finished(part, mine[-1], over_cores(part), far_last, state, far, mask))

    s = P("rollout", "dp", None)
    return jax.shard_map(
        per_device, mesh=mesh, in_specs=(s, s, s, s, s, P("rollout"), P()), out_specs=(s, s, s, P(None, "dp", None)), check_vma=False
    )
```

```python
import functools
import jax
import jax.numpy as jnp
from jax import lax
from jax.experimental import pallas as pl
from jax.experimental.pallas import tpu as pltpu
from jax.sharding import PartitionSpec as P

VMEM_SPEC = pl.BlockSpec(memory_space=pltpu.VMEM)


def turned_here(inner, outer):
    return (lax.axis_index("rollout") % 2 == 1) if inner == outer else (lax.axis_index("rollout") < 0)


def plane_peer(mine, step, count):
    return mine ^ (0 if step == 0 else (step + count - 3) % (count - 1) + 1)


def line_peer(mine, step, count):
    if count != 4:
        return (mine + step) & (count - 1)
    place = (mine & 1) * 2 + (mine >> 1)
    to = (place + (0, 1, 3, 2)[step]) & 3
    return (to & 1) * 2 + (to >> 1)


def product_kernel(inner, outer, cuts, features_hbm, upstream_hbm, *refs):
    blocks, (features, upstream, product, sems) = refs[:inner], refs[inner:]
    chunks = len(cuts) - 1
    rows = product.shape[0] // (inner * outer)
    copies = []
    for c in range(chunks):
        part = pl.ds(cuts[c], cuts[c + 1] - cuts[c])
        pair = (
            pltpu.make_async_copy(features_hbm.at[part], features.at[part], sems.at[c, 0]),
            pltpu.make_async_copy(upstream_hbm.at[part], upstream.at[part], sems.at[c, 1]),
        )
        for copy in pair:
            copy.start()
        copies.append(pair)
    turned = turned_here(inner, outer)
    mine = jnp.where(turned, lax.axis_index("dp") // inner, lax.rem(lax.axis_index("dp"), inner))
    peer_step = jnp.where(turned, inner, 1)
    other_step = jnp.where(turned, 1, inner)
    for c in range(chunks):
        part = slice(cuts[c], cuts[c + 1])
        for copy in copies[c]:
            copy.wait()
        term = lax.dot_general(
            features[part], upstream[part], (((0,), (0,)), ((), ())), preferred_element_type=jnp.float32
        )
        product[...] = term if c == 0 else product[...] + term
    for d in range(inner):
        peer = jnp.where(turned, line_peer(mine, d, inner), plane_peer(mine, d, inner))
        for o in range(0, outer, 2):
            places = [((o + i) * other_step + peer * peer_step) * rows for i in range(2)]
            parts = [product[pl.ds(pl.multiple_of(at, rows), rows), :] for at in places]
            blocks[d][o * rows : (o + 2) * rows] = jnp.concatenate(parts, axis=0).astype(jnp.bfloat16)


def product_blocks(features, upstream, inner, outer):
    tokens, rows = features.shape
    ff = upstream.shape[1]
    shares = [0, 1, 2, 3]
    unit = tokens // shares[-1]
    cuts = [share * unit for share in shares] if tokens % (16 * shares[-1]) == 0 else [0, tokens]
    block = pltpu.VMEM((rows // inner, ff), jnp.bfloat16)
    return pl.pallas_call(
        functools.partial(product_kernel, inner, outer, cuts),
        out_shape=[block] * inner,
        in_specs=[pl.BlockSpec(memory_space=pltpu.HBM)] * 2,
        out_specs=[VMEM_SPEC] * inner,
        scratch_shapes=[
            pltpu.VMEM((tokens, rows), jnp.bfloat16),
            pltpu.VMEM((tokens, ff), jnp.bfloat16),
            pltpu.VMEM((rows, ff), jnp.float32),
            pltpu.SemaphoreType.DMA((len(cuts) - 1, 2)),
        ],
        compiler_params=pltpu.CompilerParams(vmem_limit_bytes=24 * 2**20),
        name="product",
    )(*(pltpu.with_memory_space_constraint(x, pltpu.HBM) for x in (features, upstream)))


def middle_kernel(inner, outer, packs, *refs):
    got, state, sent, total = refs[:inner], refs[inner : inner + packs], refs[inner + packs : -1], refs[-1]
    acc = got[0][...].astype(jnp.float32)
    for g in got[1:]:
        acc = acc + g[...].astype(jnp.float32)
    total[...] = acc
    rows = total.shape[0] // outer
    turned = turned_here(inner, outer)
    mine = jnp.where(turned, lax.rem(lax.axis_index("dp"), inner), lax.axis_index("dp") // inner)
    for d in range(outer):
        peer = jnp.where(turned, plane_peer(mine, d, outer), line_peer(mine, d, outer))
        sent[d][:, : total.shape[1]] = total[pl.ds(pl.multiple_of(peer * rows, rows), rows), :].astype(sent[d].dtype)
    if packs:
        cross, ff = sent[outer - 1], total.shape[1]
        for k in range(2):
            cross[:, ff + k * 128 : ff + (k + 1) * 128] = jnp.broadcast_to(state[0][k], (rows, 128))


def middle_sums(got, inner, outer, state=()):
    rows, ff = got[0].shape
    part = pltpu.VMEM((rows // outer, ff), jnp.float32)
    packed = [pltpu.VMEM((rows // outer, ff + 256), jnp.float32)] if state else []
    args = held_in_vmem((*got, *state))
    return pl.pallas_call(
        functools.partial(middle_kernel, inner, outer, len(state)),
        out_shape=[part] * (outer - len(packed)) + packed,
        in_specs=[VMEM_SPEC] * len(args),
        out_specs=[VMEM_SPEC] * outer,
        scratch_shapes=[pltpu.VMEM((rows, ff), jnp.float32)],
        compiler_params=pltpu.CompilerParams(vmem_limit_bytes=8 * 2**20),
        name="middle",
    )(*args)


def stepped(grad, first, second, master, step):
    new_first = 0.9 * first[0] + 0.1 * grad
    new_second = 0.999 * second[0] + 0.001 * grad * grad
    update = new_first / step[0] / (jnp.sqrt(new_second / step[1]) + 1e-08) + 0.1 * master[0]
    return master[0] - 0.02 * update, new_first, new_second


def publish_kernel(n_parts, *refs):
    parts, state, (grad, rounded) = refs[:n_parts], refs[n_parts:-2], refs[-2:]
    acc = parts[0][...].astype(jnp.float32)
    for p in parts[1:]:
        acc = acc + p[...].astype(jnp.float32)
    grad[...] = acc
    rounded[0] = stepped(acc, *state)[0].astype(jnp.bfloat16)


def store_kernel(grad, first, second, master, step, *refs):
    outs, (held, sems) = refs[:3], refs[3:]
    copies = []
    for k, value in enumerate(stepped(grad[...], first, second, master, step)):
        held[k] = value
        copy = pltpu.make_async_copy(held.at[k], outs[k].at[0], sems.at[k])
        copy.start()
        copies.append(copy)
    for copy in copies:
        copy.wait()


def held_in_vmem(arrays):
    return [pltpu.with_memory_space_constraint(x, pltpu.VMEM) for x in arrays]


def to_publish(parts, state):
    shape = state[0].shape
    args = held_in_vmem((*parts, *state))
    return pl.pallas_call(
        functools.partial(publish_kernel, len(parts)),
        out_shape=[pltpu.VMEM(shape[1:], jnp.float32), pltpu.VMEM(shape, jnp.bfloat16)],
        in_specs=[VMEM_SPEC] * len(args),
        out_specs=[VMEM_SPEC] * 2,
        compiler_params=pltpu.CompilerParams(vmem_limit_bytes=8 * 2**20),
        name="publish",
    )(*args)


def stored(grad, state):
    shape = state[0].shape
    args = held_in_vmem((grad, *state))
    return pl.pallas_call(
        store_kernel,
        out_shape=[jax.ShapeDtypeStruct(shape, jnp.float32)] * 3,
        in_specs=[VMEM_SPEC] * len(args),
        out_specs=[pl.BlockSpec(memory_space=pltpu.HBM)] * 3,
        scratch_shapes=[pltpu.VMEM((3, *shape[1:]), jnp.float32), pltpu.SemaphoreType.DMA((3,))],
        compiler_params=pltpu.CompilerParams(vmem_limit_bytes=8 * 2**20),
        cost_estimate=pl.CostEstimate(flops=2**20, bytes_accessed=2**20, transcendentals=0),
        name="store",
    )(*args)


def pack_kernel(first, second, master, anchor, out):
    for k, ref in enumerate((first, second, master)):
        out[k] = ref[0]


def packed_state(state, anchor):
    return pl.pallas_call(
        pack_kernel,
        out_shape=pltpu.VMEM((3, *state[0].shape[1:]), jnp.float32),
        in_specs=[VMEM_SPEC] * 4,
        out_specs=VMEM_SPEC,
        compiler_params=pltpu.CompilerParams(vmem_limit_bytes=4 * 2**20),
        name="pack",
    )(*held_in_vmem((*state[:3], anchor)))


def partial_kernel(*refs):
    acc = refs[0][...]
    for ref in refs[1:-1]:
        acc = acc + ref[...]
    refs[-1][...] = acc


def partial_sum(parts):
    return pl.pallas_call(
        partial_kernel,
        out_shape=pltpu.VMEM(parts[0].shape, jnp.float32),
        in_specs=[VMEM_SPEC] * len(parts),
        out_specs=VMEM_SPEC,
        compiler_params=pltpu.CompilerParams(vmem_limit_bytes=4 * 2**20),
        name="partial",
    )(*held_in_vmem(parts))


def finish_kernel(
    part, last, far_part, far_last, first, second, master, step, far, mask, *refs
):
    outs, published, (held, rounded, sems) = refs[:3], refs[3], refs[4:]
    copies = []
    ours = stepped(part[...] + last[:, : part.shape[1]], first, second, master, step)
    for k, value in enumerate(ours):
        held[k] = value
        copy = pltpu.make_async_copy(held.at[k], outs[k].at[0], sems.at[k])
        copy.start()
        copies.append(copy)
    ff = part.shape[1]
    steps = [far_last[:, ff + k * 128 : ff + k * 128 + 1] for k in range(2)]
    theirs = stepped(far_part[...] + far_last[:, :ff], far.at[0:1], far.at[1:2], far.at[2:3], steps)[0]
    here = mask[...] > 0
    rounded[0] = jnp.where(here, ours[0], theirs).astype(jnp.bfloat16)
    rounded[1] = jnp.where(here, theirs, ours[0]).astype(jnp.bfloat16)
    copies.append(pltpu.make_async_copy(rounded, published, sems.at[3]))
    copies[-1].start()
    for copy in copies:
        copy.wait()


def finished(part, last, far_part, far_last, state, far, mask):
    shape = state[0].shape
    args = held_in_vmem((part, last, far_part, far_last, *state, far, mask))
    return pl.pallas_call(
        finish_kernel,
        out_shape=[jax.ShapeDtypeStruct(shape, jnp.float32)] * 3
        + [jax.ShapeDtypeStruct((2, *shape[1:]), jnp.bfloat16)],
        in_specs=[VMEM_SPEC] * len(args),
        out_specs=[pl.BlockSpec(memory_space=pltpu.HBM)] * 4,
        scratch_shapes=[
            pltpu.VMEM((3, *shape[1:]), jnp.float32),
            pltpu.VMEM((2, *shape[1:]), jnp.bfloat16),
            pltpu.SemaphoreType.DMA((4,)),
        ],
        compiler_params=pltpu.CompilerParams(vmem_limit_bytes=8 * 2**20),
        name="finish",
    )(*args)


def over_cores(x):
    return lax.ppermute(x, "rollout", [(0, 1), (1, 0)])


def split_of(n):
    inner = 1
    while inner * inner < n:
        inner *= 2
    return inner, n // inner


def exchange(block, step, count, level, inner, n, n_ro, cross=0):
    pairs = []
    for i in range(n):
        for r in range(n_ro):
            turned = r % 2 == 1 and inner * inner == n
            line = turned if level == 1 else not turned
            stride, rule = (inner, line_peer) if line else (1, plane_peer)
            mine = i // stride % count
            to = i + (rule(mine, step, count) - mine) * stride
            pairs.append((i * n_ro + r, to * n_ro + (r ^ cross)))
    return lax.ppermute(block, ("dp", "rollout"), pairs)


def swap(blocks, level, inner, n, n_ro):
    count = len(blocks)
    return [blocks[0]] + [exchange(blocks[k], k, count, level, inner, n, n_ro) for k in range(1, count)]


def solution(mesh):
    n_dp = mesh.shape["dp"]
    n_ro = mesh.shape["rollout"]

    def per_device(layer_inputs, cotangent, master, first_moment, second_moment, step_count, bucket_owner):
        inner, outer = split_of(n_dp)
        blocks = product_blocks(layer_inputs[0], cotangent[0], inner, outer)
        got = swap(blocks, 1, inner, n_dp, n_ro)
        counts = (step_count + 1).astype(jnp.float32)
        corrections = 1.0 - jnp.power(jnp.array([0.9, 0.999], jnp.float32), counts)
        state = (first_moment, second_moment, master, corrections[:, None, None])
        if n_ro != 2:
            parts = middle_sums(got, inner, outer)
            grad, rounded = to_publish(swap(parts, 2, inner, n_dp, n_ro), state)
            every_group = lax.all_gather(rounded, "rollout", axis=0, tiled=True)
            return (*stored(grad, state), jnp.take(every_group, bucket_owner, axis=0))
        parts = middle_sums(got, inner, outer, state[3:])
        mine = swap(parts, 2, inner, n_dp, n_ro)
        far_last = exchange(parts[-1], outer - 1, outer, 2, inner, n_dp, n_ro, cross=1)
        far = over_cores(packed_state(state, blocks[0]))
        part = partial_sum(mine[:-1])
        mask = jnp.full((1, 1), bucket_owner[0] == lax.axis_index("rollout"), jnp.float32)
        return tuple(finished(part, mine[-1], over_cores(part), far_last, state, far, mask))

    s = P("rollout", "dp", None)
    return jax.shard_map(
        per_device, mesh=mesh, in_specs=(s, s, s, s, s, P("rollout"), P()), out_specs=(s, s, s, P(None, "dp", None)), check_vma=False
    )
```
